32 devices in a mesh: row: 16 (over z, y, x), col: 2 (over core).
Axes of the slice: x: 2, y: 2, z: 4, core: 2. Of those that a mesh axis runs over, the one named last changes fastest.
Arguments:
- right_side: float32 [12288, 1280], P('row', 'col'), may hold values from -6 to 6
- factor_panel: bfloat16 [512, 3, 12288], P('col', None, 'row'), may hold values from -0.15625 to 0.15625
- diag_inverse: float32 [3, 512, 512], P(None, 'row'), may hold values from -1.5 to 1.5, as said below
Outputs:
- solved: float32 [12288, 1280], P('row', 'col')
The draws below stay inside these ranges and needn't reach their ends.
Inputs may be any that keep to these rules, and one draw needn't show every extreme that they name: `diag_inverse`: each of the 3 blocks is zero above its diagonal; its diagonal lies between 0.5 and 1.5.
All inputs are finite; a program needn't handle non-finite values.
Results may differ from the reference program's by a relative error of at most 0.003.
Values may be sent and summed in bfloat16 or wider, within the bound.
A program may use at most 64 MiB of HBM per device.

```python
import jax
import jax.numpy as jnp
from jax import lax

NB = 512
KB = 3
RD = 768
RB = 32
R = 12288
NRHS = 1280
N_ROW = 16


def draw_diag_inverse(key, part):
    first_key, second_key = jax.random.split(jax.random.fold_in(key, 17))
    lower = jax.random.uniform(first_key, (KB, NB, NB), jnp.float32, -1.0, 1.0) * jnp.sqrt(3.0 / NB)
    diag_vals = 0.5 + jax.random.uniform(second_key, (KB, NB), jnp.float32)
    row_ids = jnp.arange(NB)[:, None]
    col_ids = jnp.arange(NB)[None, :]
    strict = (row_ids > col_ids)[None, :, :]
    ident = (row_ids == col_ids)[None, :, :]
    return jnp.where(strict, lower, 0.0) + jnp.where(ident, diag_vals[:, :, None], 0.0)


def level_of(key, dims, pieces, smallest, top_value):
    factor_of, own = 1.0, jax.random.fold_in(key, 6)
    for dim, blocks in pieces:
        heights = jnp.exp(jax.random.uniform(jax.random.fold_in(own, dim), (blocks,), jnp.float32, smallest / len(pieces), top_value / len(pieces)))
        factor_of = factor_of * jnp.repeat(heights, dims[dim] // blocks).reshape([-1 if axis == dim else 1 for axis in range(len(dims))])
    return factor_of


def noise(own_key, extent, deviation, bound, shards=(), held_as=jnp.bfloat16):
    result = jax.random.normal(own_key, extent, jnp.float32) * deviation
    if len(shards) > 0:
        result = level_of(own_key, extent, shards, -0.22, 0.18) * result
    return jnp.clip(result, min=-bound, max=bound).astype(held_as)


def setup_inputs(seed: int = 0) -> dict:
    splits = jax.random.split(jax.random.key(seed), 4)
    return {
        "right_side": noise(splits[0], (R, NRHS), 1.0, 6.0, ((0, 16), (1, 2)), jnp.float32),
        "factor_panel": noise(splits[1], (NB, KB, R), (KB * NB) ** -0.5, 0.15625, ((0, 2), (2, 16))),
        "diag_inverse": draw_diag_inverse(jax.random.fold_in(splits[3], 71), 0),
    }


def reference(right_side, factor_panel, diag_inverse):
    workspace = right_side.reshape(N_ROW, RD, NRHS)
    for step_index in reversed(range(KB)):
        offset = RD - (KB - step_index) * RB
        block_rhs = workspace[:, offset:offset + RB, :].reshape(NB, NRHS)
        block_x = jnp.dot(diag_inverse[step_index].T, block_rhs, precision=lax.Precision.HIGHEST, preferred_element_type=jnp.float32)
        workspace = workspace.at[:, offset:offset + RB, :].set(block_x.reshape(N_ROW, RB, NRHS))
        block_low = lax.optimization_barrier(block_x.astype(jnp.bfloat16))
        block_wide = block_low.astype(jnp.float32)
        panel_block = factor_panel[:, step_index, :].reshape(NB, N_ROW, RD)[:, :, :offset].astype(jnp.float32)
        update = jnp.einsum("mrl,mc->rlc", panel_block, block_wide, precision=lax.Precision.HIGHEST)
        workspace = workspace.at[:, :offset, :].add(-update)
    return workspace.reshape(R, NRHS)
```

```python
import functools

import jax
import jax.numpy as jnp
from jax import lax
from jax.experimental import pallas as pl
from jax.experimental.pallas import tpu as pltpu
from jax.sharding import PartitionSpec as P

KB = 3
MESH = pl.DeviceIdType.MESH
LANES = 128
PAIRS = ((2, 1), (2, 0), (1, 0))


def shards(right_side, factor_panel, diag_inverse):
    local_rows = right_side.shape[0]
    block_rows = diag_inverse.shape[1]
    workspace = right_side
    for step_index in reversed(range(KB)):
        offset = local_rows - (KB - step_index) * block_rows
        block_rhs = workspace[offset : offset + block_rows]
        partial_value = lax.dot_general(
            diag_inverse[step_index],
            block_rhs,
            (((0,), (0,)), ((), ())),
            precision=lax.Precision.HIGHEST,
            preferred_element_type=jnp.float32,
        )
        whole_x = lax.psum(partial_value, "row")
        own_rows = lax.dynamic_slice_in_dim(
            whole_x, lax.axis_index("row") * block_rows, block_rows, 0
        )
        block_low = whole_x.astype(jnp.bfloat16)
        update = lax.dot_general(
            lax.all_gather(factor_panel[:, step_index, :offset], "col", axis=0, tiled=True),
            block_low,
            (((0,), (0,)), ((), ())),
            preferred_element_type=jnp.float32,
        )
        workspace = jnp.concatenate(
            [workspace[:offset] - update, own_rows, workspace[offset + block_rows :]], axis=0
        )
    return workspace


def nt_dot(left, right):
    return lax.dot_general(
        left, right, (((1,), (1,)), ((), ())), preferred_element_type=jnp.float32
    )


def kernel(
    outer, inner,
    rhs_ref, ft_ref, dinv_ref, out_ref,
    ftx, dg, fg, xg, xt, bts, btr, yts, ytr,
    s1_send, s1_recv, s2_send, s2_recv, sib_send, sib_recv, a2a_send, a2a_recv,
):
    n_row = outer * inner
    me = lax.axis_index("row")
    core = lax.axis_index("col")
    z, p = me // inner, me % inner
    rows, _ = rhs_ref.shape
    block = dinv_ref.shape[1]
    half = ft_ref.shape[2]
    chunk = bts.shape[1]
    kept = rows - KB * block
    window = rows - LANES

    barrier = pltpu.get_barrier_semaphore()
    for d in range(1, n_row):
        pl.semaphore_signal(
            barrier, inc=1, device_id={"row": lax.rem(me + d, n_row)}, device_id_type=MESH
        )
    pl.semaphore_signal(barrier, inc=1, device_id={"col": 1 - core}, device_id_type=MESH)

    lanes = pl.ds(pl.multiple_of(core * half, half), half)
    for k in range(KB):
        dg[core, k, z, p] = dinv_ref[k, :, lanes]
    for pair, (k, j) in enumerate(PAIRS):
        fg[core, pair, z, p] = ft_ref[k, kept + j * block : kept + (j + 1) * block, :]
    bts[...] = rhs_ref[window:, :].T.reshape(n_row, chunk, LANES)
    btr[me] = bts[me]

    pl.semaphore_wait(barrier, n_row)

    pending = []

    def remote(src, dst, send_sem, recv_sem, device_id):
        return pltpu.make_async_remote_copy(
            src_ref=src, dst_ref=dst, send_sem=send_sem, recv_sem=recv_sem,
            device_id=device_id, device_id_type=MESH,
        )

    def view(item):
        kind, i = item
        if kind == "d":
            return i, dg.at[core, i]
        if kind == "f":
            return KB + i, fg.at[core, i]
        return 2 * KB + i, xg.at[i]

    def first(item):
        n, ref = view(item)
        copies = []
        for d in range(1, outer):
            c = remote(
                ref.at[z, p], ref.at[z, p], s1_send.at[n, d], s1_recv.at[n, d],
                {"row": lax.rem(z + d, outer) * inner + p},
            )
            c.start()
            pending.append(c)
            copies.append(c)
        return copies

    def second(item, copies):
        for c in copies:
            c.wait_recv()
        n, ref = view(item)
        copies = []
        for d in range(1, inner):
            c = remote(
                ref.at[:, p], ref.at[:, p], s2_send.at[n, d], s2_recv.at[n, d],
                {"row": z * inner + lax.rem(p + d, inner)},
            )
            c.start()
            pending.append(c)
            copies.append(c)
        return copies

    def to_sibling(item, copies):
        for c in copies:
            c.wait_recv()
        n, ref = view(item)
        c = remote(ref, ref, sib_send.at[n], sib_recv.at[n], {"col": 1 - core})
        c.start()
        pending.append(c)
        return c

    def all_to_all(src, dst, which):
        copies = []
        for d in range(1, n_row):
            to = lax.rem(me + d, n_row)
            c = remote(
                src.at[to], dst.at[me], a2a_send.at[which, d], a2a_recv.at[which, d], {"row": to}
            )
            c.start()
            pending.append(c)
            copies.append(c)
        return copies

    order = [("d", 2), ("f", 0), ("d", 1), ("f", 1), ("f", 2), ("d", 0)]
    arrive = {}
    arrive[order[0]] = first(order[0])
    b_copies = all_to_all(bts, btr, 0)
    for item in order[1:]:
        arrive[item] = first(item)
    ft_copy = remote(
        ft_ref, ftx, sib_send.at[2 * KB], sib_recv.at[2 * KB], {"col": 1 - core}
    )
    ft_copy.start()
    pending.append(ft_copy)

    lane_group = lax.broadcasted_iota(jnp.int32, (chunk, LANES), 1) // block
    per_tile = LANES // block

    def gathered_rhs(k):
        tiles = []
        for g in range(n_row // per_tile):
            total = jnp.zeros((chunk, LANES), jnp.float32)
            for q in range(per_tile):
                shift = (block * q - (LANES - (KB - k) * block)) % LANES
                part = btr[per_tile * g + q]
                if shift:
                    part = pltpu.roll(part, shift, 1)
                total = jnp.where(lane_group == q, part, total)
            tiles.append(total)
        return jnp.concatenate(tiles, axis=1)

    def solve(k, w):
        halves = []
        for h in range(2):
            halves.append(
                jnp.dot(
                    w, dg[h, k].reshape(n_row * block, half),
                    precision=lax.Precision.HIGHEST, preferred_element_type=jnp.float32,
                )
            )
        xg[k, z, p] = jnp.concatenate(halves, axis=0).astype(jnp.bfloat16)
        return halves

    def couple(pair, halves):
        total = None
        for h in range(2):
            term = nt_dot(
                halves[h].astype(jnp.bfloat16), fg[h, pair].reshape(n_row * block, half)
            )
            total = term if total is None else total + term
        return total

    for item in order[:3]:
        arrive[item] = second(item, arrive[item])
    sib = {}
    sib[order[0]] = to_sibling(order[0], arrive[order[0]])
    for item in order[3:]:
        arrive[item] = second(item, arrive[item])
    for c in b_copies:
        c.wait_recv()
    w2 = gathered_rhs(2)
    w1 = gathered_rhs(1)
    w0 = gathered_rhs(0)
    sib[order[0]].wait_recv()
    x2 = solve(2, w2)
    a2 = first(("x", 2))
    for item in order[1:3]:
        sib[item] = to_sibling(item, arrive[item])
    sib[("f", 0)].wait_recv()
    w1 = w1 - couple(0, x2)
    sib[("d", 1)].wait_recv()
    x1 = solve(1, w1)
    a1 = first(("x", 1))
    a2 = second(("x", 2), a2)
    for item in order[3:]:
        sib[item] = to_sibling(item, arrive[item])
    sib[("f", 1)].wait_recv()
    w0 = w0 - couple(1, x2)
    sib[("f", 2)].wait_recv()
    w0 = w0 - couple(2, x1)
    sib[("d", 0)].wait_recv()
    x0 = solve(0, w0)
    a0 = first(("x", 0))

    whole = [jnp.concatenate(x, axis=1) for x in (x0, x1, x2)]
    for r in range(n_row):
        g, q = r // per_tile, r % per_tile
        total = jnp.zeros((chunk, LANES), jnp.float32)
        for k in range(KB):
            start = LANES - (KB - k) * block
            part = whole[k][:, g * LANES : (g + 1) * LANES]
            shift = (start - block * q) % LANES
            if shift:
                part = pltpu.roll(part, shift, 1)
            total = jnp.where(lane_group == start // block, part, total)
        yts[r] = total
    ytr[me] = yts[me]
    a1 = second(("x", 1), a1)
    y_copies = all_to_all(yts, ytr, 1)
    a0 = second(("x", 0), a0)

    tiles = 3
    tile = kept // tiles

    def update(k, copies, base):
        for c in copies:
            c.wait_recv()
        v = xg[k].reshape(n_row, 2 * chunk, half).astype(jnp.float32)
        for h in range(2):
            xt[h] = v[:, h * chunk : (h + 1) * chunk].reshape(n_row * chunk, half).astype(
                jnp.bfloat16
            )

        @pl.loop(0, tiles)
        def _(t):
            at = pl.ds(pl.multiple_of(t * tile, tile), tile)
            out_ref[at, :] = (
                base[at, :] - nt_dot(ft_ref[k, at, :], xt[core]) - nt_dot(ftx[k, at, :], xt[1 - core])
            )

    ft_copy.wait_recv()
    update(2, a2, rhs_ref)
    update(1, a1, out_ref)
    update(0, a0, out_ref)
    for c in y_copies:
        c.wait_recv()
    out_ref[kept:, :] = ytr[...].reshape(n_row * chunk, LANES).T[LANES - KB * block :, :]
    for c in pending:
        c.wait_send()


def fused(outer, inner, right_side, factor_panel, diag_inverse):
    rows, columns = right_side.shape
    half = factor_panel.shape[0]
    block = diag_inverse.shape[1]
    n_row = outer * inner
    chunk = columns // n_row
    panel = jnp.transpose(factor_panel, (1, 2, 0))
    vmem = pl.BlockSpec(memory_space=pltpu.VMEM)
    dma = pltpu.SemaphoreType.DMA
    square = (2, KB, outer, inner, block, half)
    return pl.pallas_call(
        functools.partial(kernel, outer, inner),
        out_shape=jax.ShapeDtypeStruct((rows, columns), jnp.float32),
        in_specs=[vmem] * 3,
        out_specs=vmem,
        scratch_shapes=[
            pltpu.VMEM((KB, rows, half), jnp.bfloat16),
            pltpu.VMEM(square, jnp.float32),
            pltpu.VMEM(square, jnp.bfloat16),
            pltpu.VMEM((KB, outer, inner, 2 * chunk, half), jnp.bfloat16),
            pltpu.VMEM((2, columns, half), jnp.bfloat16),
            pltpu.VMEM((n_row, chunk, LANES), jnp.float32),
            pltpu.VMEM((n_row, chunk, LANES), jnp.float32),
            pltpu.VMEM((n_row, chunk, LANES), jnp.float32),
            pltpu.VMEM((n_row, chunk, LANES), jnp.float32),
            dma((3 * KB, outer)),
            dma((3 * KB, outer)),
            dma((3 * KB, inner)),
            dma((3 * KB, inner)),
            dma((2 * KB + 1,)),
            dma((2 * KB + 1,)),
            dma((2, n_row)),
            dma((2, n_row)),
        ],
        compiler_params=pltpu.CompilerParams(
            collective_id=0, has_side_effects=True, vmem_limit_bytes=48 * 1024 * 1024
        ),
        cost_estimate=pl.CostEstimate(
            flops=2 * KB * rows * columns * 2 * half, bytes_accessed=8 * rows * columns,
            transcendentals=0,
        ),
    )(right_side, panel, diag_inverse)


def solution(mesh):
    n_row, n_col = mesh.shape["row"], mesh.shape["col"]
    inner = 4
    placed = (P("row", "col"), P("col", None, "row"), P(None, "row", None))
    body = shards
    if n_col == 2 and n_row == 16:
        body = functools.partial(fused, n_row // inner, inner)
    return jax.shard_map(
        body, mesh=mesh, in_specs=placed, out_specs=P("row", "col"), check_vma=False
    )
```

```python
import functools

import jax
import jax.numpy as jnp
from jax import lax
from jax.experimental import pallas as pl
from jax.experimental.pallas import tpu as pltpu
from jax.sharding import PartitionSpec as P

KB = 3
MESH = pl.DeviceIdType.MESH
LANES = 128
PAIRS = ((2, 1), (2, 0), (1, 0))
UNITS = (
    ((0, 0), (1, 0)),
    ((1, 0), (2, 0)),
    ((2, 0), (3, 0)),
    ((3, 0), (2, 1)),
    ((3, 1), (3, 1)),
)


def shards(right_side, factor_panel, diag_inverse):
    local_rows = right_side.shape[0]
    block_rows = diag_inverse.shape[1]
    workspace = right_side
    for step_index in reversed(range(KB)):
        offset = local_rows - (KB - step_index) * block_rows
        block_rhs = workspace[offset : offset + block_rows]
        partial_value = lax.dot_general(
            diag_inverse[step_index],
            block_rhs,
            (((0,), (0,)), ((), ())),
            precision=lax.Precision.HIGHEST,
            preferred_element_type=jnp.float32,
        )
        whole_x = lax.psum(partial_value, "row")
        own_rows = lax.dynamic_slice_in_dim(
            whole_x, lax.axis_index("row") * block_rows, block_rows, 0
        )
        block_low = whole_x.astype(jnp.bfloat16)
        update = lax.dot_general(
            lax.all_gather(factor_panel[:, step_index, :offset], "col", axis=0, tiled=True),
            block_low,
            (((0,), (0,)), ((), ())),
            preferred_element_type=jnp.float32,
        )
        workspace = jnp.concatenate(
            [workspace[:offset] - update, own_rows, workspace[offset + block_rows :]], axis=0
        )
    return workspace


def nt_dot(left, right):
    return lax.dot_general(
        left, right, (((1,), (1,)), ((), ())), preferred_element_type=jnp.float32
    )


def kernel(
    outer, inner,
    rhs_ref, ft_ref, dinv_ref, out_ref,
    ftx, ds, dg, fg, xg, xt, bts, btr, yts, ytr,
    s1_send, s1_recv, s2_send, s2_recv, sib_send, sib_recv, a2a_send, a2a_recv,
):
    n_row = outer * inner
    me = lax.axis_index("row")
    core = lax.axis_index("col")
    z, p = me // inner, me % inner
    rows, _ = rhs_ref.shape
    block = dinv_ref.shape[1]
    half = ft_ref.shape[2]
    chunk = bts.shape[1]
    kept = rows - KB * block
    window = rows - LANES

    barrier = pltpu.get_barrier_semaphore()
    for d in range(1, n_row):
        pl.semaphore_signal(
            barrier, inc=1, device_id={"row": lax.rem(me + d, n_row)}, device_id_type=MESH
        )
    pl.semaphore_signal(barrier, inc=1, device_id={"col": 1 - core}, device_id_type=MESH)

    low = pl.ds(pl.multiple_of(core * LANES, LANES), LANES)
    high = pl.ds(pl.multiple_of((outer - 1 - core) * LANES, LANES), LANES)
    for k in range(KB):
        ds[k, z, 0] = dinv_ref[k, :, low]
        ds[k, z, 1] = dinv_ref[k, :, high]
    for pair, (k, j) in enumerate(PAIRS):
        fg[core, pair, z, p] = ft_ref[k, kept + j * block : kept + (j + 1) * block, :]
    bts[...] = rhs_ref[window:, :].T.reshape(n_row, chunk, LANES)
    btr[me] = bts[me]

    pl.semaphore_wait(barrier, n_row)

    pending = []

    def remote(src, dst, send_sem, recv_sem, device_id):
        return pltpu.make_async_remote_copy(
            src_ref=src, dst_ref=dst, send_sem=send_sem, recv_sem=recv_sem,
            device_id=device_id, device_id_type=MESH,
        )

    along_x = p + 1 - 2 * (p % 2)
    along_y = p + 2 - 4 * (p // 2)
    near = along_x * (1 - core) + along_y * core
    far = along_y * (1 - core) + along_x * core

    def view(item):
        kind, i = item
        if kind == "d":
            return i, dg.at[core, i]
        if kind == "f":
            return KB + i, fg.at[core, i]
        return 2 * KB + i, xg.at[i]

    def first(item):
        kind, i = item
        n, ref = view(item)
        own = ds.at[i, z] if kind == "d" else ref.at[z, p]
        copies = []
        for d in range(1, outer):
            c = remote(
                own, own, s1_send.at[n, d], s1_recv.at[n, d],
                {"row": lax.rem(z + d, outer) * inner + p},
            )
            c.start()
            pending.append(c)
            copies.append(c)
        return copies

    def in_plane(item, slot, way, to):
        n, ref = view(item)
        c = remote(
            ref.at[:, slot], ref.at[:, slot], s2_send.at[n, way], s2_recv.at[n, way],
            {"row": z * inner + to},
        )
        c.start()
        pending.append(c)
        return c

    def second(item, copies):
        for c in copies:
            c.wait_recv()
        kind, k = item
        if kind == "d":
            for u, ((z0, g0), (z1, g1)) in enumerate(UNITS):
                dg[core, k, u, p] = ds[k, z0 + core * (z1 - z0), g0 + core * (g1 - g0)]
        return [in_plane(item, p, 0, near), in_plane(item, p, 1, far)]

    def third(item, copies):
        copies[0].wait_recv()
        return [copies[1], in_plane(item, near, 2, far)]

    def to_sibling(item, copies):
        for c in copies:
            c.wait_recv()
        n, ref = view(item)
        c = remote(ref, ref, sib_send.at[n], sib_recv.at[n], {"col": 1 - core})
        c.start()
        pending.append(c)
        return c

    def all_to_all(src, dst, which):
        copies = []
        for d in range(1, n_row):
            to = lax.rem(me + d, n_row)
            c = remote(
                src.at[to], dst.at[me], a2a_send.at[which, d], a2a_recv.at[which, d], {"row": to}
            )
            c.start()
            pending.append(c)
            copies.append(c)
        return copies

    order = [("d", 2), ("f", 0), ("d", 1), ("f", 1), ("f", 2), ("d", 0)]
    arrive = {}
    arrive[order[0]] = first(order[0])
    b_copies = all_to_all(bts, btr, 0)
    for item in order[1:]:
        arrive[item] = first(item)
    ft_copy = remote(
        ft_ref, ftx, sib_send.at[2 * KB], sib_recv.at[2 * KB], {"col": 1 - core}
    )
    ft_copy.start()
    pending.append(ft_copy)

    lane_group = lax.broadcasted_iota(jnp.int32, (chunk, LANES), 1) // block
    per_tile = LANES // block

    def gathered_rhs(k):
        tiles = []
        for g in range(n_row // per_tile):
            total = jnp.zeros((chunk, LANES), jnp.float32)
            for q in range(per_tile):
                shift = (block * q - (LANES - (KB - k) * block)) % LANES
                part = btr[per_tile * g + q]
                if shift:
                    part = pltpu.roll(part, shift, 1)
                total = jnp.where(lane_group == q, part, total)
            tiles.append(total)
        return jnp.concatenate(tiles, axis=1)

    def solve(k, w):
        def group(side, units):
            part = dg[side, k, units].reshape(-1, LANES)
            return jnp.dot(
                w[:, w.shape[1] - part.shape[0] :], part,
                precision=lax.Precision.HIGHEST, preferred_element_type=jnp.float32,
            )

        halves = [
            jnp.concatenate([group(0, slice(0, 4)), group(1, slice(0, 3))], axis=1),
            jnp.concatenate([group(1, slice(3, 5)), group(0, slice(4, 5))], axis=1),
        ]
        xg[k, z, p] = jnp.concatenate(halves, axis=0).astype(jnp.bfloat16)
        return halves

    def couple(pair, halves):
        total = None
        for h in range(2):
            term = nt_dot(
                halves[h].astype(jnp.bfloat16), fg[h, pair].reshape(n_row * block, half)
            )
            total = term if total is None else total + term
        return total

    for item in order[:2]:
        arrive[item] = second(item, arrive[item])
    arrive[order[0]] = third(order[0], arrive[order[0]])
    arrive[order[2]] = second(order[2], arrive[order[2]])
    arrive[order[1]] = third(order[1], arrive[order[1]])
    sib = {}
    sib[order[0]] = to_sibling(order[0], arrive[order[0]])
    for c in b_copies:
        c.wait_recv()
    w2 = gathered_rhs(2)
    w1 = gathered_rhs(1)
    w0 = gathered_rhs(0)
    sib[order[0]].wait_recv()
    x2 = solve(2, w2)
    a2 = first(("x", 2))
    for item in order[3:]:
        arrive[item] = second(item, arrive[item])
    for item in order[2:]:
        arrive[item] = third(item, arrive[item])
    a2 = second(("x", 2), a2)
    for item in order[1:3]:
        sib[item] = to_sibling(item, arrive[item])
    sib[("f", 0)].wait_recv()
    w1 = w1 - couple(0, x2)
    sib[("d", 1)].wait_recv()
    x1 = solve(1, w1)
    a1 = first(("x", 1))
    for item in order[3:]:
        sib[item] = to_sibling(item, arrive[item])
    a2 = third(("x", 2), a2)
    a1 = second(("x", 1), a1)
    sib[("f", 1)].wait_recv()
    w0 = w0 - couple(1, x2)
    sib[("f", 2)].wait_recv()
    w0 = w0 - couple(2, x1)
    sib[("d", 0)].wait_recv()
    x0 = solve(0, w0)
    a0 = first(("x", 0))
    a1 = third(("x", 1), a1)

    whole = [jnp.concatenate(x, axis=1) for x in (x0, x1, x2)]
    for r in range(n_row):
        g, q = r // per_tile, r % per_tile
        total = jnp.zeros((chunk, LANES), jnp.float32)
        for k in range(KB):
            start = LANES - (KB - k) * block
            part = whole[k][:, g * LANES : (g + 1) * LANES]
            shift = (start - block * q) % LANES
            if shift:
                part = pltpu.roll(part, shift, 1)
            total = jnp.where(lane_group == start // block, part, total)
        yts[r] = total
    ytr[me] = yts[me]
    y_copies = all_to_all(yts, ytr, 1)
    a0 = second(("x", 0), a0)

    tiles = 3
    tile = kept // tiles

    def update(k, copies, base):
        for c in copies:
            c.wait_recv()
        v = xg[k].reshape(n_row, 2 * chunk, half).astype(jnp.float32)
        for h in range(2):
            xt[h] = v[:, h * chunk : (h + 1) * chunk].reshape(n_row * chunk, half).astype(
                jnp.bfloat16
            )

        @pl.loop(0, tiles)
        def _(t):
            at = pl.ds(pl.multiple_of(t * tile, tile), tile)
            out_ref[at, :] = (
                base[at, :] - nt_dot(ft_ref[k, at, :], xt[core]) - nt_dot(ftx[k, at, :], xt[1 - core])
            )

    ft_copy.wait_recv()
    update(2, a2, rhs_ref)
    a0 = third(("x", 0), a0)
    update(1, a1, out_ref)
    update(0, a0, out_ref)
    for c in y_copies:
        c.wait_recv()
    out_ref[kept:, :] = ytr[...].reshape(n_row * chunk, LANES).T[LANES - KB * block :, :]
    for c in pending:
        c.wait_send()


def fused(outer, inner, right_side, factor_panel, diag_inverse):
    rows, columns = right_side.shape
    half = factor_panel.shape[0]
    block = diag_inverse.shape[1]
    n_row = outer * inner
    chunk = columns // n_row
    panel = jnp.transpose(factor_panel, (1, 2, 0))
    vmem = pl.BlockSpec(memory_space=pltpu.VMEM)
    dma = pltpu.SemaphoreType.DMA
    square = (2, KB, outer, inner, block, half)
    packed = (2, KB, len(UNITS), inner, block, LANES)
    return pl.pallas_call(
        functools.partial(kernel, outer, inner),
        out_shape=jax.ShapeDtypeStruct((rows, columns), jnp.float32),
        in_specs=[vmem] * 3,
        out_specs=vmem,
        scratch_shapes=[
            pltpu.VMEM((KB, rows, half), jnp.bfloat16),
            pltpu.VMEM((KB, outer, 2, block, LANES), jnp.float32),
            pltpu.VMEM(packed, jnp.float32),
            pltpu.VMEM(square, jnp.bfloat16),
            pltpu.VMEM((KB, outer, inner, 2 * chunk, half), jnp.bfloat16),
            pltpu.VMEM((2, columns, half), jnp.bfloat16),
            pltpu.VMEM((n_row, chunk, LANES), jnp.float32),
            pltpu.VMEM((n_row, chunk, LANES), jnp.float32),
            pltpu.VMEM((n_row, chunk, LANES), jnp.float32),
            pltpu.VMEM((n_row, chunk, LANES), jnp.float32),
            dma((3 * KB, outer)),
            dma((3 * KB, outer)),
            dma((3 * KB, 3)),
            dma((3 * KB, 3)),
            dma((2 * KB + 1,)),
            dma((2 * KB + 1,)),
            dma((2, n_row)),
            dma((2, n_row)),
        ],
        compiler_params=pltpu.CompilerParams(
            collective_id=0, has_side_effects=True, vmem_limit_bytes=48 * 1024 * 1024
        ),
        cost_estimate=pl.CostEstimate(
            flops=2 * KB * rows * columns * 2 * half, bytes_accessed=8 * rows * columns,
            transcendentals=0,
        ),
    )(right_side, panel, diag_inverse)


def solution(mesh):
    n_row, n_col = mesh.shape["row"], mesh.shape["col"]
    inner = 4
    placed = (P("row", "col"), P("col", None, "row"), P(None, "row", None))
    body = shards
    if n_col == 2 and n_row == 16:
        body = functools.partial(fused, n_row // inner, inner)
    return jax.shard_map(
        body, mesh=mesh, in_specs=placed, out_specs=P("row", "col"), check_vma=False
    )
```

```python
import functools

import jax
import jax.numpy as jnp
from jax import lax
from jax.experimental import pallas as pl
from jax.experimental.pallas import tpu as pltpu
from jax.sharding import PartitionSpec as P

KB = 3
MESH = pl.DeviceIdType.MESH
LANES = 128
PAIRS = ((2, 1), (2, 0), (1, 0))
UNITS = (
    ((0, 0), (1, 0)),
    ((1, 0), (2, 0)),
    ((2, 0), (3, 0)),
    ((3, 0), (2, 1)),
    ((3, 1), (3, 1)),
)


def shards(right_side, factor_panel, diag_inverse):
    local_rows = right_side.shape[0]
    block_rows = diag_inverse.shape[1]
    workspace = right_side
    for step_index in reversed(range(KB)):
        offset = local_rows - (KB - step_index) * block_rows
        block_rhs = workspace[offset : offset + block_rows]
        partial_value = lax.dot_general(
            diag_inverse[step_index],
            block_rhs,
            (((0,), (0,)), ((), ())),
            precision=lax.Precision.HIGHEST,
            preferred_element_type=jnp.float32,
        )
        whole_x = lax.psum(partial_value, "row")
        own_rows = lax.dynamic_slice_in_dim(
            whole_x, lax.axis_index("row") * block_rows, block_rows, 0
        )
        block_low = whole_x.astype(jnp.bfloat16)
        update = lax.dot_general(
            lax.all_gather(factor_panel[:, step_index, :offset], "col", axis=0, tiled=True),
            block_low,
            (((0,), (0,)), ((), ())),
            preferred_element_type=jnp.float32,
        )
        workspace = jnp.concatenate(
            [workspace[:offset] - update, own_rows, workspace[offset + block_rows :]], axis=0
        )
    return workspace


def nt_dot(left, right):
    return lax.dot_general(
        left, right, (((1,), (1,)), ((), ())), preferred_element_type=jnp.float32
    )


def kernel(
    outer, inner,
    rhs_ref, ft_ref, dinv_ref, out_ref,
    ftx, ds, dg, fg, xg, xt, bts, btr, yts, ytr,
    s1_send, s1_recv, s2_send, s2_recv, sib_send, sib_recv, a2a_send, a2a_recv,
):
    n_row = outer * inner
    me = lax.axis_index("row")
    core = lax.axis_index("col")
    z, p = me // inner, me % inner
    rows, _ = rhs_ref.shape
    block = dinv_ref.shape[1]
    half = ft_ref.shape[2]
    chunk = bts.shape[1]
    kept = rows - KB * block
    window = rows - LANES

    barrier = pltpu.get_barrier_semaphore()
    for d in range(1, n_row):
        pl.semaphore_signal(
            barrier, inc=1, device_id={"row": lax.rem(me + d, n_row)}, device_id_type=MESH
        )
    pl.semaphore_signal(barrier, inc=1, device_id={"col": 1 - core}, device_id_type=MESH)

    low = pl.ds(pl.multiple_of(core * LANES, LANES), LANES)
    high = pl.ds(pl.multiple_of((outer - 1 - core) * LANES, LANES), LANES)
    for k in range(KB):
        ds[k, z, 0] = dinv_ref[k, :, low]
        ds[k, z, 1] = dinv_ref[k, :, high]
    for pair, (k, j) in enumerate(PAIRS):
        fg[core, pair, z, p] = ft_ref[k, kept + j * block : kept + (j + 1) * block, :]
    bts[...] = rhs_ref[window:, :].T.reshape(n_row, chunk, LANES)
    btr[me] = bts[me]

    pl.semaphore_wait(barrier, n_row)

    pending = []

    def remote(src, dst, send_sem, recv_sem, device_id):
        return pltpu.make_async_remote_copy(
            src_ref=src, dst_ref=dst, send_sem=send_sem, recv_sem=recv_sem,
            device_id=device_id, device_id_type=MESH,
        )

    along_x = p + 1 - 2 * (p % 2)
    along_y = p + 2 - 4 * (p // 2)
    near = along_x * (1 - core) + along_y * core
    far = along_y * (1 - core) + along_x * core

    def view(item):
        kind, lo, hi = item
        if kind == "d":
            return lo, dg.at[core, lo:hi]
        if kind == "f":
            return KB + lo, fg.at[core, lo:hi]
        return 2 * KB + lo, xg.at[lo:hi]

    def first(item):
        kind, lo, hi = item
        n, ref = view(item)
        own = ds.at[lo:hi, z] if kind == "d" else ref.at[:, z, p]
        copies = []
        for d in range(1, outer):
            c = remote(
                own, own, s1_send.at[n, d], s1_recv.at[n, d],
                {"row": lax.rem(z + d, outer) * inner + p},
            )
            c.start()
            pending.append(c)
            copies.append(c)
        return copies

    def in_plane(item, slot, way, to):
        n, ref = view(item)
        c = remote(
            ref.at[:, :, slot], ref.at[:, :, slot], s2_send.at[n, way], s2_recv.at[n, way],
            {"row": z * inner + to},
        )
        c.start()
        pending.append(c)
        return c

    def second(item, copies):
        for c in copies:
            c.wait_recv()
        kind, lo, hi = item
        for k in range(lo, hi) if kind == "d" else ():
            for u, ((z0, g0), (z1, g1)) in enumerate(UNITS):
                dg[core, k, u, p] = ds[k, z0 + core * (z1 - z0), g0 + core * (g1 - g0)]
        return [in_plane(item, p, 0, near), in_plane(item, p, 1, far)]

    def third(item, copies):
        copies[0].wait_recv()
        return [copies[1], in_plane(item, near, 2, far)]

    def to_sibling(item, copies):
        for c in copies:
            c.wait_recv()
        n, ref = view(item)
        c = remote(ref, ref, sib_send.at[n], sib_recv.at[n], {"col": 1 - core})
        c.start()
        pending.append(c)
        return c

    def all_to_all(src, dst, which):
        copies = []
        for d in range(1, n_row):
            to = lax.rem(me + d, n_row)
            c = remote(
                src.at[to], dst.at[me], a2a_send.at[which, d], a2a_recv.at[which, d], {"row": to}
            )
            c.start()
            pending.append(c)
            copies.append(c)
        return copies

    order = [("d", 2, 3), ("f", 0, 1), ("d", 1, 2), ("f", 1, 3), ("d", 0, 1)]
    s2, s1, s0 = ("x", 2, 3), ("x", 1, 2), ("x", 0, 1)
    arrive = {}
    arrive[order[0]] = first(order[0])
    b_copies = all_to_all(bts, btr, 0)
    arrive[order[1]] = first(order[1])
    ft_copy = remote(
        ft_ref, ftx, sib_send.at[2 * KB], sib_recv.at[2 * KB], {"col": 1 - core}
    )
    ft_copy.start()
    pending.append(ft_copy)

    lane_group = lax.broadcasted_iota(jnp.int32, (chunk, LANES), 1) // block
    per_tile = LANES // block

    def gathered_rhs(k):
        tiles = []
        for g in range(n_row // per_tile):
            total = jnp.zeros((chunk, LANES), jnp.float32)
            for q in range(per_tile):
                shift = (block * q - (LANES - (KB - k) * block)) % LANES
                part = btr[per_tile * g + q]
                if shift:
                    part = pltpu.roll(part, shift, 1)
                total = jnp.where(lane_group == q, part, total)
            tiles.append(total)
        return jnp.concatenate(tiles, axis=1)

    def solve(k, w):
        def group(side, units):
            part = dg[side, k, units].reshape(-1, LANES)
            return jnp.dot(
                w[:, w.shape[1] - part.shape[0] :], part,
                precision=lax.Precision.HIGHEST, preferred_element_type=jnp.float32,
            )

        halves = [
            jnp.concatenate([group(0, slice(0, 4)), group(1, slice(0, 3))], axis=1),
            jnp.concatenate([group(1, slice(3, 5)), group(0, slice(4, 5))], axis=1),
        ]
        xg[k, z, p] = jnp.concatenate(halves, axis=0).astype(jnp.bfloat16)
        return halves

    def couple(pair, halves):
        total = None
        for h in range(2):
            term = nt_dot(
                halves[h].astype(jnp.bfloat16), fg[h, pair].reshape(n_row * block, half)
            )
            total = term if total is None else total + term
        return total

    arrive[order[0]] = second(order[0], arrive[order[0]])
    arrive[order[2]] = first(order[2])
    arrive[order[1]] = second(order[1], arrive[order[1]])
    arrive[order[3]] = first(order[3])
    arrive[order[0]] = third(order[0], arrive[order[0]])
    arrive[order[2]] = second(order[2], arrive[order[2]])
    arrive[order[4]] = first(order[4])
    arrive[order[1]] = third(order[1], arrive[order[1]])
    sib = {}
    sib[order[0]] = to_sibling(order[0], arrive[order[0]])
    for c in b_copies:
        c.wait_recv()
    w2 = gathered_rhs(2)
    w1 = gathered_rhs(1)
    w0 = gathered_rhs(0)
    sib[order[0]].wait_recv()
    x2 = solve(2, w2)
    a2 = first(s2)
    arrive[order[3]] = second(order[3], arrive[order[3]])
    arrive[order[2]] = third(order[2], arrive[order[2]])
    sib[order[1]] = to_sibling(order[1], arrive[order[1]])
    arrive[order[4]] = second(order[4], arrive[order[4]])
    a2 = second(s2, a2)
    sib[order[1]].wait_recv()
    w1 = w1 - couple(0, x2)
    sib[order[2]] = to_sibling(order[2], arrive[order[2]])
    arrive[order[3]] = third(order[3], arrive[order[3]])
    sib[order[2]].wait_recv()
    x1 = solve(1, w1)
    a1 = first(s1)
    arrive[order[4]] = third(order[4], arrive[order[4]])
    sib[order[3]] = to_sibling(order[3], arrive[order[3]])
    a2 = third(s2, a2)
    sib[order[3]].wait_recv()
    w0 = w0 - couple(1, x2)
    w0 = w0 - couple(2, x1)
    a1 = second(s1, a1)
    sib[order[4]] = to_sibling(order[4], arrive[order[4]])
    sib[order[4]].wait_recv()
    x0 = solve(0, w0)
    a0 = first(s0)
    a1 = third(s1, a1)

    whole = [jnp.concatenate(x, axis=1) for x in (x0, x1, x2)]
    for r in range(n_row):
        g, q = r // per_tile, r % per_tile
        total = jnp.zeros((chunk, LANES), jnp.float32)
        for k in range(KB):
            start = LANES - (KB - k) * block
            part = whole[k][:, g * LANES : (g + 1) * LANES]
            shift = (start - block * q) % LANES
            if shift:
                part = pltpu.roll(part, shift, 1)
            total = jnp.where(lane_group == start // block, part, total)
        yts[r] = total
    ytr[me] = yts[me]
    a0 = second(s0, a0)
    y_copies = all_to_all(yts, ytr, 1)

    tiles = 3
    tile = kept // tiles

    def update(k, copies, base):
        for c in copies:
            c.wait_recv()
        v = xg[k].reshape(n_row, 2 * chunk, half).astype(jnp.float32)
        for h in range(2):
            xt[h] = v[:, h * chunk : (h + 1) * chunk].reshape(n_row * chunk, half).astype(
                jnp.bfloat16
            )

        @pl.loop(0, tiles)
        def _(t):
            at = pl.ds(pl.multiple_of(t * tile, tile), tile)
            out_ref[at, :] = (
                base[at, :] - nt_dot(ft_ref[k, at, :], xt[core]) - nt_dot(ftx[k, at, :], xt[1 - core])
            )

    ft_copy.wait_recv()
    update(2, a2, rhs_ref)
    a0 = third(s0, a0)
    update(1, a1, out_ref)
    update(0, a0, out_ref)
    for c in y_copies:
        c.wait_recv()
    out_ref[kept:, :] = ytr[...].reshape(n_row * chunk, LANES).T[LANES - KB * block :, :]
    for c in pending:
        c.wait_send()


def fused(outer, inner, right_side, factor_panel, diag_inverse):
    rows, columns = right_side.shape
    half = factor_panel.shape[0]
    block = diag_inverse.shape[1]
    n_row = outer * inner
    chunk = columns // n_row
    panel = jnp.transpose(factor_panel, (1, 2, 0))
    vmem = pl.BlockSpec(memory_space=pltpu.VMEM)
    dma = pltpu.SemaphoreType.DMA
    square = (2, KB, outer, inner, block, half)
    packed = (2, KB, len(UNITS), inner, block, LANES)
    return pl.pallas_call(
        functools.partial(kernel, outer, inner),
        out_shape=jax.ShapeDtypeStruct((rows, columns), jnp.float32),
        in_specs=[vmem] * 3,
        out_specs=vmem,
        scratch_shapes=[
            pltpu.VMEM((KB, rows, half), jnp.bfloat16),
            pltpu.VMEM((KB, outer, 2, block, LANES), jnp.float32),
            pltpu.VMEM(packed, jnp.float32),
            pltpu.VMEM(square, jnp.bfloat16),
            pltpu.VMEM((KB, outer, inner, 2 * chunk, half), jnp.bfloat16),
            pltpu.VMEM((2, columns, half), jnp.bfloat16),
            pltpu.VMEM((n_row, chunk, LANES), jnp.float32),
            pltpu.VMEM((n_row, chunk, LANES), jnp.float32),
            pltpu.VMEM((n_row, chunk, LANES), jnp.float32),
            pltpu.VMEM((n_row, chunk, LANES), jnp.float32),
            dma((3 * KB, outer)),
            dma((3 * KB, outer)),
            dma((3 * KB, 3)),
            dma((3 * KB, 3)),
            dma((2 * KB + 1,)),
            dma((2 * KB + 1,)),
            dma((2, n_row)),
            dma((2, n_row)),
        ],
        compiler_params=pltpu.CompilerParams(
            collective_id=0, has_side_effects=True, vmem_limit_bytes=48 * 1024 * 1024
        ),
        cost_estimate=pl.CostEstimate(
            flops=2 * KB * rows * columns * 2 * half, bytes_accessed=8 * rows * columns,
            transcendentals=0,
        ),
    )(right_side, panel, diag_inverse)


def solution(mesh):
    n_row, n_col = mesh.shape["row"], mesh.shape["col"]
    inner = 4
    placed = (P("row", "col"), P("col", None, "row"), P(None, "row", None))
    body = shards
    if n_col == 2 and n_row == 16:
        body = functools.partial(fused, n_row // inner, inner)
    return jax.shard_map(
        body, mesh=mesh, in_specs=placed, out_specs=P("row", "col"), check_vma=False
    )
```

```python
import functools

import jax
import jax.numpy as jnp
from jax import lax
from jax.experimental import pallas as pl
from jax.experimental.pallas import tpu as pltpu
from jax.sharding import PartitionSpec as P

KB = 3
MESH = pl.DeviceIdType.MESH
LANES = 128
PAIRS = ((2, 1), (2, 0), (1, 0))
UNITS = (
    ((0, 0), (1, 0)),
    ((1, 0), (2, 0)),
    ((2, 0), (3, 0)),
    ((3, 0), (2, 1)),
    ((3, 1), (3, 1)),
)


def shards(right_side, factor_panel, diag_inverse):
    local_rows = right_side.shape[0]
    block_rows = diag_inverse.shape[1]
    workspace = right_side
    for step_index in reversed(range(KB)):
        offset = local_rows - (KB - step_index) * block_rows
        block_rhs = workspace[offset : offset + block_rows]
        partial_value = lax.dot_general(
            diag_inverse[step_index],
            block_rhs,
            (((0,), (0,)), ((), ())),
            precision=lax.Precision.HIGHEST,
            preferred_element_type=jnp.float32,
        )
        whole_x = lax.psum(partial_value, "row")
        own_rows = lax.dynamic_slice_in_dim(
            whole_x, lax.axis_index("row") * block_rows, block_rows, 0
        )
        block_low = whole_x.astype(jnp.bfloat16)
        update = lax.dot_general(
            lax.all_gather(factor_panel[:, step_index, :offset], "col", axis=0, tiled=True),
            block_low,
            (((0,), (0,)), ((), ())),
            preferred_element_type=jnp.float32,
        )
        workspace = jnp.concatenate(
            [workspace[:offset] - update, own_rows, workspace[offset + block_rows :]], axis=0
        )
    return workspace


def nt_dot(left, right):
    return lax.dot_general(
        left, right, (((1,), (1,)), ((), ())), preferred_element_type=jnp.float32
    )


def kernel(
    outer, inner,
    rhs_ref, ft_ref, dinv_ref, out_ref,
    ftx, ds, dg, fg, xg, xt, bts, btr, yts, ytr,
    s1_send, s1_recv, s2_send, s2_recv, sib_send, sib_recv, a2a_send, a2a_recv,
):
    n_row = outer * inner
    me = lax.axis_index("row")
    core = lax.axis_index("col")
    z, p = me // inner, me % inner
    rows, _ = rhs_ref.shape
    block = dinv_ref.shape[1]
    half = ft_ref.shape[2]
    chunk = bts.shape[1]
    kept = rows - KB * block
    window = rows - LANES

    barrier = pltpu.get_barrier_semaphore()
    for d in range(1, n_row):
        pl.semaphore_signal(
            barrier, inc=1, device_id={"row": lax.rem(me + d, n_row)}, device_id_type=MESH
        )
    pl.semaphore_signal(barrier, inc=1, device_id={"col": 1 - core}, device_id_type=MESH)

    low = pl.ds(pl.multiple_of(core * LANES, LANES), LANES)
    high = pl.ds(pl.multiple_of((outer - 1 - core) * LANES, LANES), LANES)
    for k in range(KB):
        ds[k, z, 0] = dinv_ref[k, :, low]
        ds[k, z, 1] = dinv_ref[k, :, high]
    for pair, (k, j) in enumerate(PAIRS):
        fg[core, pair, z, p] = ft_ref[k, kept + j * block : kept + (j + 1) * block, :]
    bts[...] = rhs_ref[window:, :].T.reshape(n_row, chunk, LANES)
    btr[me] = bts[me]

    pl.semaphore_wait(barrier, n_row)

    pending = []

    def remote(src, dst, send_sem, recv_sem, device_id):
        return pltpu.make_async_remote_copy(
            src_ref=src, dst_ref=dst, send_sem=send_sem, recv_sem=recv_sem,
            device_id=device_id, device_id_type=MESH,
        )

    along_x = p + 1 - 2 * (p % 2)
    along_y = p + 2 - 4 * (p // 2)
    near = along_x * (1 - core) + along_y * core
    far = along_y * (1 - core) + along_x * core

    def view(item):
        kind, lo, hi = item
        if kind == "d":
            return lo, dg.at[core, lo:hi]
        if kind == "f":
            return KB + lo, fg.at[core, lo:hi]
        return 2 * KB + lo, xg.at[lo:hi]

    def first(item):
        kind, lo, hi = item
        n, ref = view(item)
        own = ds.at[lo:hi, z] if kind == "d" else ref.at[:, z, p]
        copies = []
        for d in range(1, outer):
            c = remote(
                own, own, s1_send.at[n, d], s1_recv.at[n, d],
                {"row": lax.rem(z + d, outer) * inner + p},
            )
            c.start()
            pending.append(c)
            copies.append(c)
        return copies

    def in_plane(item, slot, way, to):
        n, ref = view(item)
        c = remote(
            ref.at[:, :, slot], ref.at[:, :, slot], s2_send.at[n, way], s2_recv.at[n, way],
            {"row": z * inner + to},
        )
        c.start()
        pending.append(c)
        return c

    def second(item, copies):
        for c in copies:
            c.wait_recv()
        kind, lo, hi = item
        for k in range(lo, hi) if kind == "d" else ():
            for u, ((z0, g0), (z1, g1)) in enumerate(UNITS):
                dg[core, k, u, p] = ds[k, z0 + core * (z1 - z0), g0 + core * (g1 - g0)]
        return [in_plane(item, p, 0, near), in_plane(item, p, 1, far)]

    def third(item, copies):
        copies[0].wait_recv()
        return [copies[1], in_plane(item, near, 2, far)]

    def to_sibling(item, copies):
        for c in copies:
            c.wait_recv()
        n, ref = view(item)
        c = remote(ref, ref, sib_send.at[n], sib_recv.at[n], {"col": 1 - core})
        c.start()
        pending.append(c)
        return c

    def all_to_all(src, dst, which):
        copies = []
        for d in range(1, n_row):
            to = lax.rem(me + d, n_row)
            c = remote(
                src.at[to], dst.at[me], a2a_send.at[which, d], a2a_recv.at[which, d], {"row": to}
            )
            c.start()
            pending.append(c)
            copies.append(c)
        return copies

    order = [("d", 2, 3), ("f", 0, 1), ("d", 1, 2), ("f", 1, 3), ("d", 0, 1)]
    s2, s1, s0 = ("x", 2, 3), ("x", 1, 2), ("x", 0, 1)
    arrive = {}
    arrive[order[0]] = first(order[0])
    b_copies = all_to_all(bts, btr, 0)
    arrive[order[1]] = first(order[1])
    ft_copy = remote(
        ft_ref, ftx, sib_send.at[2 * KB], sib_recv.at[2 * KB], {"col": 1 - core}
    )
    ft_copy.start()
    pending.append(ft_copy)

    lane_group = lax.broadcasted_iota(jnp.int32, (chunk, LANES), 1) // block
    per_tile = LANES // block

    def gathered_rhs(k):
        tiles = []
        for g in range(n_row // per_tile):
            total = jnp.zeros((chunk, LANES), jnp.float32)
            for q in range(per_tile):
                shift = (block * q - (LANES - (KB - k) * block)) % LANES
                part = btr[per_tile * g + q]
                if shift:
                    part = pltpu.roll(part, shift, 1)
                total = jnp.where(lane_group == q, part, total)
            tiles.append(total)
        return jnp.concatenate(tiles, axis=1)

    def solve(k, w):
        def group(side, units):
            part = dg[side, k, units].reshape(-1, LANES)
            return jnp.dot(
                w[:, w.shape[1] - part.shape[0] :], part,
                precision=lax.Precision.HIGHEST, preferred_element_type=jnp.float32,
            )

        halves = [
            jnp.concatenate([group(0, slice(0, 4)), group(1, slice(0, 3))], axis=1),
            jnp.concatenate([group(1, slice(3, 5)), group(0, slice(4, 5))], axis=1),
        ]
        xg[k, z, p] = jnp.concatenate(halves, axis=0).astype(jnp.bfloat16)
        return halves

    def couple(pair, halves):
        total = None
        for h in range(2):
            term = nt_dot(
                halves[h].astype(jnp.bfloat16), fg[h, pair].reshape(n_row * block, half)
            )
            total = term if total is None else total + term
        return total

    arrive[order[0]] = second(order[0], arrive[order[0]])
    arrive[order[2]] = first(order[2])
    arrive[order[1]] = second(order[1], arrive[order[1]])
    arrive[order[3]] = first(order[3])
    arrive[order[0]] = third(order[0], arrive[order[0]])
    arrive[order[2]] = second(order[2], arrive[order[2]])
    arrive[order[4]] = first(order[4])
    arrive[order[1]] = third(order[1], arrive[order[1]])
    sib = {}
    sib[order[0]] = to_sibling(order[0], arrive[order[0]])
    for c in b_copies:
        c.wait_recv()
    w2 = gathered_rhs(2)
    w1 = gathered_rhs(1)
    w0 = gathered_rhs(0)
    sib[order[0]].wait_recv()
    x2 = solve(2, w2)
    a2 = first(s2)
    arrive[order[3]] = second(order[3], arrive[order[3]])
    arrive[order[2]] = third(order[2], arrive[order[2]])
    sib[order[1]] = to_sibling(order[1], arrive[order[1]])
    arrive[order[4]] = second(order[4], arrive[order[4]])
    a2 = second(s2, a2)
    sib[order[1]].wait_recv()
    w1 = w1 - couple(0, x2)
    sib[order[2]] = to_sibling(order[2], arrive[order[2]])
    arrive[order[3]] = third(order[3], arrive[order[3]])
    sib[order[2]].wait_recv()
    x1 = solve(1, w1)
    a1 = first(s1)
    arrive[order[4]] = third(order[4], arrive[order[4]])
    sib[order[3]] = to_sibling(order[3], arrive[order[3]])
    a2 = third(s2, a2)
    sib[order[3]].wait_recv()
    w0 = w0 - couple(1, x2)
    w0 = w0 - couple(2, x1)
    a1 = second(s1, a1)
    sib[order[4]] = to_sibling(order[4], arrive[order[4]])
    sib[order[4]].wait_recv()
    x0 = solve(0, w0)
    a0 = first(s0)
    a1 = third(s1, a1)

    tiles = 3
    tile = kept // tiles

    def update(k, copies, base):
        for c in copies:
            c.wait_recv()
        v = xg[k].reshape(n_row, 2 * chunk, half).astype(jnp.float32)
        for h in range(2):
            xt[h] = v[:, h * chunk : (h + 1) * chunk].reshape(n_row * chunk, half).astype(
                jnp.bfloat16
            )

        @pl.loop(0, tiles)
        def _(t):
            at = pl.ds(pl.multiple_of(t * tile, tile), tile)
            out_ref[at, :] = (
                base[at, :] - nt_dot(ft_ref[k, at, :], xt[core]) - nt_dot(ftx[k, at, :], xt[1 - core])
            )

    whole = [jnp.concatenate(x, axis=1) for x in (x0, x1, x2)]
    for r in range(n_row):
        g, q = r // per_tile, r % per_tile
        total = jnp.zeros((chunk, LANES), jnp.float32)
        for k in range(KB):
            start = LANES - (KB - k) * block
            part = whole[k][:, g * LANES : (g + 1) * LANES]
            shift = (start - block * q) % LANES
            if shift:
                part = pltpu.roll(part, shift, 1)
            total = jnp.where(lane_group == start // block, part, total)
        yts[r] = total
    ytr[me] = yts[me]
    ft_copy.wait_recv()
    update(2, a2, rhs_ref)
    a0 = second(s0, a0)
    y_copies = all_to_all(yts, ytr, 1)

    a0 = third(s0, a0)
    update(1, a1, out_ref)
    update(0, a0, out_ref)
    for c in y_copies:
        c.wait_recv()
    out_ref[kept:, :] = ytr[...].reshape(n_row * chunk, LANES).T[LANES - KB * block :, :]
    for c in pending:
        c.wait_send()


def fused(outer, inner, right_side, factor_panel, diag_inverse):
    rows, columns = right_side.shape
    half = factor_panel.shape[0]
    block = diag_inverse.shape[1]
    n_row = outer * inner
    chunk = columns // n_row
    panel = jnp.transpose(factor_panel, (1, 2, 0))
    vmem = pl.BlockSpec(memory_space=pltpu.VMEM)
    dma = pltpu.SemaphoreType.DMA
    square = (2, KB, outer, inner, block, half)
    packed = (2, KB, len(UNITS), inner, block, LANES)
    return pl.pallas_call(
        functools.partial(kernel, outer, inner),
        out_shape=jax.ShapeDtypeStruct((rows, columns), jnp.float32),
        in_specs=[vmem] * 3,
        out_specs=vmem,
        scratch_shapes=[
            pltpu.VMEM((KB, rows, half), jnp.bfloat16),
            pltpu.VMEM((KB, outer, 2, block, LANES), jnp.float32),
            pltpu.VMEM(packed, jnp.float32),
            pltpu.VMEM(square, jnp.bfloat16),
            pltpu.VMEM((KB, outer, inner, 2 * chunk, half), jnp.bfloat16),
            pltpu.VMEM((2, columns, half), jnp.bfloat16),
            pltpu.VMEM((n_row, chunk, LANES), jnp.float32),
            pltpu.VMEM((n_row, chunk, LANES), jnp.float32),
            pltpu.VMEM((n_row, chunk, LANES), jnp.float32),
            pltpu.VMEM((n_row, chunk, LANES), jnp.float32),
            dma((3 * KB, outer)),
            dma((3 * KB, outer)),
            dma((3 * KB, 3)),
            dma((3 * KB, 3)),
            dma((2 * KB + 1,)),
            dma((2 * KB + 1,)),
            dma((2, n_row)),
            dma((2, n_row)),
        ],
        compiler_params=pltpu.CompilerParams(
            collective_id=0, has_side_effects=True, vmem_limit_bytes=48 * 1024 * 1024
        ),
        cost_estimate=pl.CostEstimate(
            flops=2 * KB * rows * columns * 2 * half, bytes_accessed=8 * rows * columns,
            transcendentals=0,
        ),
    )(right_side, panel, diag_inverse)


def solution(mesh):
    n_row, n_col = mesh.shape["row"], mesh.shape["col"]
    inner = 4
    placed = (P("row", "col"), P("col", None, "row"), P(None, "row", None))
    body = shards
    if n_col == 2 and n_row == 16:
        body = functools.partial(fused, n_row // inner, inner)
    return jax.shard_map(
        body, mesh=mesh, in_specs=placed, out_specs=P("row", "col"), check_vma=False
    )
```
